32 devices in a mesh: req: 16 (over z, y, core), head: 2 (over x).
Axes of the slice: x: 2, y: 2, z: 4, core: 2. Of those that a mesh axis runs over, the one named last changes fastest.
Arguments:
- queries: bfloat16 [64, 8192], P('req', 'head'), may hold values from -200 to 200
- new_kv: bfloat16 [2, 64, 1024], P(None, 'req', 'head'), may hold values from -6 to 6
- own_kv: bfloat16 [2, 512, 64, 1024], P(None, 'req', None, 'head'), may hold values from -6 to 6
- man_kv: bfloat16 [2, 32, 64, 1024], P(None, 'req', None, 'head'), may hold values from -6 to 6
- pages: int32 [64, 8], P('req'), may hold values from 0 to 31
- own_len: int32 [64], P('req'), may hold values from 1 to 8, as said below
- resid: bfloat16 [64, 8192], P(None, 'req'), may hold values from -3 to 3
- w_out: bfloat16 [8192, 8192], P('head', 'req'), may hold values from -0.8984375 to 0.8984375
- w_gate: bfloat16 [8192, 14336], P('req', 'head'), may hold values from -0.0625 to 0.0625
- w_up: bfloat16 [8192, 14336], P('req', 'head'), may hold values from -0.0625 to 0.0625
Outputs:
- resid_out: bfloat16 [64, 8192], P(None, 'req')
- hidden: bfloat16 [64, 14336], P('req', 'head')
The draws below stay inside these ranges and needn't reach their ends.
Inputs may be any that keep to these rules, and one draw needn't show every extreme that they name: `pages`: entries at and past a request's length are padding. `own_len`: among the 4 requests of each index of req one has 8 pages.
All inputs are finite; a program needn't handle non-finite values.
Results may differ from the reference program's by a relative error of at most 0.03.
Values may be sent and summed in bfloat16 or wider, within the bound.
A program may use at most 64 MiB of HBM per device.

```python
import jax
import jax.numpy as jnp
from jax import lax

D = 8192
HEADS = 64
KVH = 8
HD = 128
FF = 14336
PAGE = 64
MAXP = 8
REQ_DEV = 4
GROUP = 8
POOL_DEV = 32
REQS = 64
MANP = 32
N_REQ = 16


def draw_queries(key, part):
    base = jax.random.normal(key, (REQS, HEADS * HD), jnp.float32) * 1.5
    return jnp.clip(base, -200.0, 200.0).astype(jnp.bfloat16)


def draw_own_len(key, part):
    blocks = REQS // REQ_DEV
    lengths = jax.random.randint(key, (REQS,), 1, MAXP + 1)
    chosen = jax.random.randint(jax.random.fold_in(key, 5), (blocks,), 0, REQ_DEV)
    where = jnp.arange(blocks, dtype=jnp.int32) * REQ_DEV + chosen
    return lengths.at[where].set(MAXP).astype(jnp.int32)


def place_ends(array, stream_key, low, top_value):
    longest = array.shape.index(max(array.shape))
    spots = []
    for shift in (0, 1):
        where = [jax.random.randint(jax.random.fold_in(stream_key, axis), (), 0, length) for axis, length in enumerate(array.shape)]
        where[longest] = (where[longest] + shift) % array.shape[longest]
        spots.append(tuple(where))
    return array.at[spots[0]].set(low).at[spots[1]].set(top_value)


def level_of(rng, extent, cuts, smallest, high):
    gain = 1.0
    for dim, parts in cuts:
        heights = jax.random.uniform(jax.random.fold_in(jax.random.fold_in(rng, 6), dim), (parts,), jnp.float32, smallest / len(cuts), high / len(cuts))
        gain = gain * jnp.repeat(jnp.exp(heights), extent[dim] // parts).reshape((-1,) + (1,) * (len(extent) - 1 - dim))
    return gain


def normal_values(stream_key, dims, scale, bound, split=(), held_as=jnp.bfloat16):
    array = jax.random.normal(stream_key, dims, jnp.float32) * scale
    if len(split) > 0:
        array = level_of(stream_key, dims, split, -0.22, 0.18) * array
    return jnp.clip(array, min=-bound, max=bound).astype(held_as)


def setup_inputs(seed: int = 0) -> dict:
    arg_keys = jax.random.split(jax.random.key(seed), 11)
    queries = draw_queries(jax.random.fold_in(arg_keys[10], 71), 0)
    new_kv = normal_values(arg_keys[1], (2, REQS, KVH * HD), 1.0, 6.0, ((1, 16), (2, 2)))
    own_kv = normal_values(arg_keys[2], (2, POOL_DEV * N_REQ, PAGE, KVH * HD), 1.0, 6.0, ((1, 16), (3, 2)))
    man_kv = normal_values(arg_keys[3], (2, MANP, PAGE, KVH * HD), 1.0, 6.0, ((1, 16), (3, 2)))
    pages = place_ends(jax.random.randint(arg_keys[4], (REQS, MAXP), 0, POOL_DEV), jax.random.fold_in(arg_keys[4], 1), 0, POOL_DEV - 1).astype(jnp.int32)
    own_len = draw_own_len(jax.random.fold_in(arg_keys[10], 71), 0)
    resid = normal_values(arg_keys[6], (REQS, D), 0.5, 3.0, ((1, 16),))
    w_out = normal_values(arg_keys[7], (HEADS * HD, D), 0.15, 0.8984375, ((0, 2), (1, 16)))
    w_gate = normal_values(arg_keys[8], (D, FF), D ** -0.5, 0.0625, ((0, 16), (1, 2)))
    w_up = normal_values(arg_keys[9], (D, FF), D ** -0.5, 0.0625, ((0, 16), (1, 2)))
    return dict(queries=queries, new_kv=new_kv, own_kv=own_kv, man_kv=man_kv, pages=pages, own_len=own_len, resid=resid, w_out=w_out, w_gate=w_gate, w_up=w_up)


def reference(queries, new_kv, own_kv, man_kv, pages, own_len, resid, w_out, w_gate, w_up):
    scale = HD ** -0.5
    q_all = queries.reshape(REQS, KVH, GROUP, HD)
    owner = (jnp.arange(REQS, dtype=jnp.int32) // REQ_DEV) * POOL_DEV
    global_pages = (owner[:, None] + pages).astype(jnp.int32)
    valid = jnp.arange(MAXP, dtype=jnp.int32)[None, :] < own_len[:, None]
    valid = jnp.repeat(valid, PAGE, axis=1)
    own_heads = own_kv.reshape(2, POOL_DEV * N_REQ, PAGE, KVH, HD)
    man_heads = man_kv.reshape(2, MANP * PAGE, KVH, HD)
    new_heads = new_kv.reshape(2, REQS, KVH, HD)

    def one_head(index):
        q_head = lax.dynamic_index_in_dim(q_all, index, 1, keepdims=False).astype(jnp.float32)
        man_k = lax.dynamic_index_in_dim(man_heads[0], index, 1, keepdims=False).astype(jnp.float32)
        man_v = lax.dynamic_index_in_dim(man_heads[1], index, 1, keepdims=False).astype(jnp.float32)
        pool_k = lax.dynamic_index_in_dim(own_heads[0], index, 2, keepdims=False)
        pool_v = lax.dynamic_index_in_dim(own_heads[1], index, 2, keepdims=False)
        own_k = pool_k[global_pages].reshape(REQS, MAXP * PAGE, HD).astype(jnp.float32)
        own_v = pool_v[global_pages].reshape(REQS, MAXP * PAGE, HD).astype(jnp.float32)
        new_k = lax.dynamic_index_in_dim(new_heads[0], index, 1, keepdims=False).astype(jnp.float32)
        new_v = lax.dynamic_index_in_dim(new_heads[1], index, 1, keepdims=False).astype(jnp.float32)
        s_man = jnp.einsum('bgd,td->bgt', q_head, man_k) * scale
        s_own = jnp.einsum('bgd,btd->bgt', q_head, own_k) * scale
        s_own = jnp.where(valid[:, None, :], s_own, -jnp.inf)
        s_new = jnp.einsum('bgd,bd->bg', q_head, new_k) * scale
        top = jnp.maximum(jnp.maximum(s_man.max(-1), s_own.max(-1)), s_new)
        p_man = jnp.exp(s_man - top[..., None])
        p_own = jnp.exp(s_own - top[..., None])
        p_new = jnp.exp(s_new - top)
        total = p_man.sum(-1) + p_own.sum(-1) + p_new
        b_man = p_man.astype(jnp.bfloat16).astype(jnp.float32)
        b_own = p_own.astype(jnp.bfloat16).astype(jnp.float32)
        b_new = p_new.astype(jnp.bfloat16).astype(jnp.float32)
        acc = jnp.einsum('bgt,td->bgd', b_man, man_v) + jnp.einsum('bgt,btd->bgd', b_own, own_v)
        acc = acc + b_new[..., None] * new_v[:, None, :]
        return (acc / total[..., None]).astype(jnp.bfloat16)

    head_split = lax.map(one_head, jnp.arange(KVH, dtype=jnp.int32))
    attn = jnp.transpose(head_split, (1, 0, 2, 3)).reshape(REQS, HEADS * HD)
    projected_rows = jnp.dot(attn, w_out, preferred_element_type=jnp.float32)
    resid_out = (resid.astype(jnp.float32) + projected_rows).astype(jnp.bfloat16)
    gate = jnp.dot(resid_out, w_gate, preferred_element_type=jnp.float32)
    up = jnp.dot(resid_out, w_up, preferred_element_type=jnp.float32)
    hidden = (jax.nn.silu(gate) * up).astype(jnp.bfloat16)
    return resid_out, hidden
```

```python
import functools

import jax
import jax.numpy as jnp
from jax import lax
from jax.experimental import pallas as pl
from jax.experimental.pallas import tpu as pltpu
from jax.sharding import PartitionSpec as P

HD = 128
PAGE = 64
MAXP = 8
GROUP = 8
CORES = 2
BF = jnp.bfloat16
F32 = jnp.float32
NT = (((1,), (1,)), ((), ()))
NN = (((1,), (0,)), ((), ()))


def grid_of(n_req):
    chips = n_req // CORES
    b = 1
    while b * 2 * b * 2 <= chips:
        b *= 2
    while chips % b:
        b -= 1
    return chips // b, b


def kernel(
    n_req, n_head, jn, cw,
    pages, own_len, queries, new_kv, man, resid, own_hbm, wo_hbm, wg_hbm, wu_hbm,
    out_ref, hid_ref,
    pool, wo, wg, wu, qf, qbuf, ksib, bias, nf, sbuf, rbuf, abuf, af, amat, dbuf,
    rf, rn, xb, pf, e1s, e1r, e2f, e2s, e2r, e3f, e3s, e3r,
    lsem, kv_s, kv_r, q_s, q_r, p_s, p_r, c_s, c_r, f_s, f_r, d_s, d_r,
    e1_ss, e1_rs, e2_ss, e2_rs, e3_ss, e3_rs,
):
    A, B = grid_of(n_req)
    NC = A * B
    kv = man.shape[2] // HD
    rows = queries.shape[0]
    blk = rows * GROUP
    width = wg.shape[1]
    scale = HD ** (-0.5)

    me = lax.axis_index("req")
    hd = lax.axis_index("head")
    core = lax.rem(me, CORES)
    chip = me // CORES
    a = chip // B
    b = lax.rem(chip, B)
    cp = b * A + a

    def dev(cp_, core_):
        return {"req": (lax.rem(cp_, A) * B + cp_ // A) * CORES + core_, "head": hd}

    def remote(src, dst, ss, rs, to):
        return pltpu.make_async_remote_copy(
            src_ref=src, dst_ref=dst, send_sem=ss, recv_sem=rs,
            device_id=to, device_id_type=pl.DeviceIdType.MESH,
        )

    sib = dev(cp, 1 - core)
    peers = [lax.rem(cp + i, NC) for i in range(NC)]
    froms = [lax.rem(cp + NC - i, NC) for i in range(NC)]

    barrier = pltpu.get_barrier_semaphore()

    def greet(to):
        pl.semaphore_signal(barrier, inc=1, device_id=to, device_id_type=pl.DeviceIdType.MESH)

    greet(sib)
    for i in range(1, NC):
        greet(dev(peers[i], core))
    for h in range(1, n_head):
        greet({"req": me, "head": lax.rem(hd + h, n_head)})

    loads = [
        pltpu.make_async_copy(own_hbm.at[0], pool.at[0], lsem.at[0]),
        pltpu.make_async_copy(own_hbm.at[1], pool.at[1], lsem.at[1]),
        pltpu.make_async_copy(wo_hbm, wo, lsem.at[2]),
        pltpu.make_async_copy(wg_hbm, wg, lsem.at[3]),
        pltpu.make_async_copy(wu_hbm, wu, lsem.at[4]),
    ]
    for c in loads:
        c.start()

    qv = queries[...].astype(F32)
    for k in range(kv):
        for g in range(GROUP):
            lane = (k * GROUP + g) * HD
            qf[pl.ds(k * blk + g, rows, stride=GROUP), :] = qv[:, lane:lane + HD]
    qbuf[cp] = qf[...].astype(BF)

    pl.semaphore_wait(barrier, 1 + (NC - 1) + (n_head - 1))

    kv_copy = remote(man, ksib, kv_s, kv_r, sib)
    kv_copy.start()
    q_out = [remote(qbuf.at[cp], qbuf.at[cp], q_s.at[i], q_r.at[i], dev(peers[i], core)) for i in range(1, NC)]
    for c in q_out:
        c.start()

    toks = pool.shape[1]
    tok_page = lax.broadcasted_iota(jnp.int32, (GROUP, toks), 1) // PAGE
    for r in range(rows):
        cnt = jnp.zeros((GROUP, toks), F32)
        for i in range(MAXP):
            pid = jnp.where(i < own_len[r], pages[r, i], -1)
            cnt = cnt + jnp.where(tok_page == pid, 1.0, 0.0)
        bias[r * GROUP:(r + 1) * GROUP, :] = jnp.where(cnt > 0.0, jnp.log(jnp.maximum(cnt, 1.0)), -1e30)
    for t in range(2):
        nv = new_kv[t].astype(F32)
        for k in range(kv):
            for g in range(GROUP):
                nf[t, pl.ds(k * blk + g, rows, stride=GROUP), :] = nv[:, k * HD:(k + 1) * HD]
    loads[0].wait()
    loads[1].wait()
    own = []
    for k in range(kv):
        rs = slice(k * blk, (k + 1) * blk)
        ls = slice(k * HD, (k + 1) * HD)
        s = lax.dot_general(qf[rs].astype(BF), pool[0, :, ls], NT, preferred_element_type=F32) * scale + bias[...]
        s_new = jnp.sum(qf[rs] * nf[0, rs], axis=1, keepdims=True) * scale
        m = jnp.maximum(jnp.max(s, axis=1, keepdims=True), s_new)
        p = jnp.exp(s - m)
        e_new = jnp.exp(s_new - m)
        l = jnp.sum(p, axis=1, keepdims=True) + e_new
        acc = lax.dot_general(p.astype(BF), pool[1, :, ls], NN, preferred_element_type=F32)
        acc = acc + e_new.astype(BF).astype(F32) * nf[1, rs]
        own.append((m, l, acc))

    kv_copy.wait()
    for i in range(1, NC):
        remote(qbuf.at[froms[i]], qbuf.at[froms[i]], q_s.at[i], q_r.at[i], dev(peers[i], core)).wait()
    lane = lax.broadcasted_iota(jnp.int32, (NC * blk, HD), 1)
    stats = jnp.zeros((NC * blk, HD), F32)
    for k in range(kv):
        ls = slice(k * HD, (k + 1) * HD)
        q = qbuf[:, k * blk:(k + 1) * blk, :].reshape(NC * blk, HD)
        s0 = lax.dot_general(q, man[0, :, ls], NT, preferred_element_type=F32) * scale
        s1 = lax.dot_general(q, ksib[0, :, ls], NT, preferred_element_type=F32) * scale
        m = jnp.maximum(jnp.max(s0, axis=1, keepdims=True), jnp.max(s1, axis=1, keepdims=True))
        m = m.astype(BF).astype(F32)
        p0 = jnp.exp(s0 - m)
        p1 = jnp.exp(s1 - m)
        l = jnp.sum(p0, axis=1, keepdims=True) + jnp.sum(p1, axis=1, keepdims=True)
        acc = lax.dot_general(p0.astype(BF), man[1, :, ls], NN, preferred_element_type=F32)
        acc = acc + lax.dot_general(p1.astype(BF), ksib[1, :, ls], NN, preferred_element_type=F32)
        sbuf[:, k * blk:(k + 1) * blk, :] = acc.astype(BF).reshape(NC, blk, HD)
        l_hi = l.astype(BF).astype(F32)
        stats = jnp.where(lane == k, m, stats)
        stats = jnp.where(lane == kv + k, l_hi, stats)
        stats = jnp.where(lane == 2 * kv + k, l - l_hi, stats)
    sbuf[:, kv * blk:(kv + 1) * blk, :] = stats.astype(BF).reshape(NC, blk, HD)
    p_out = [remote(sbuf.at[peers[i]], rbuf.at[cp], p_s.at[i], p_r.at[i], dev(peers[i], core)) for i in range(1, NC)]
    for c in p_out:
        c.start()
    rbuf[cp] = sbuf[cp]
    for i in range(1, NC):
        remote(sbuf.at[peers[i]], rbuf.at[froms[i]], p_s.at[i], p_r.at[i], dev(peers[i], core)).wait()

    st = [rbuf[n, kv * blk:(kv + 1) * blk, :].astype(F32) for n in range(NC)]
    mine = core * NC + cp
    for k in range(kv):
        rs = slice(k * blk, (k + 1) * blk)
        m, l, acc = own[k]
        top = m
        for n in range(NC):
            top = jnp.maximum(top, st[n][:, k:k + 1])
        f = jnp.exp(m - top)
        l = l * f
        acc = acc * f
        for n in range(NC):
            f = jnp.exp(st[n][:, k:k + 1] - top)
            l = l + f * (st[n][:, kv + k:kv + k + 1] + st[n][:, 2 * kv + k:2 * kv + k + 1])
            acc = acc + f * rbuf[n, rs, :].astype(F32)
        abuf[mine, rs, :] = (acc / l).astype(BF)
    slot = abuf.at[mine]
    fwd = [remote(slot, slot, f_s.at[0], f_r.at[0], sib)]
    fwd[0].start()
    c_out = [remote(slot, slot, c_s.at[i], c_r.at[i], dev(peers[i], core)) for i in range(1, NC)]
    for c in c_out:
        c.start()
    for i in range(1, NC):
        got = abuf.at[core * NC + froms[i]]
        remote(got, got, c_s.at[i], c_r.at[i], dev(peers[i], core)).wait_recv()
        c = remote(got, got, f_s.at[i], f_r.at[i], sib)
        c.start()
        fwd.append(c)

    rv = resid[...].astype(F32)
    order = [(ai * B + bi) * CORES + ci for ci in range(CORES) for bi in range(B) for ai in range(A)]
    for pos, nat in enumerate(order):
        rf[pos * rows:(pos + 1) * rows, :] = rv[nat * rows:(nat + 1) * rows, :]
    for i in range(NC):
        got = abuf.at[(1 - core) * NC + froms[i]]
        remote(got, got, f_s.at[i], f_r.at[i], sib).wait_recv()

    all_rows = n_req * rows
    for k in range(kv):
        af[k] = abuf[:, k * blk:(k + 1) * blk, :].astype(F32).reshape(n_req * blk, HD)
    for k in range(kv):
        for g in range(GROUP):
            lane0 = (k * GROUP + g) * HD
            amat[:, lane0:lane0 + HD] = af[k, pl.ds(g, all_rows, stride=GROUP), :].astype(BF)
    loads[2].wait()
    part = lax.dot_general(amat[...], wo[...], NN, preferred_element_type=F32)
    dbuf[hd] = part.astype(BF)
    d_out = []
    for h in range(1, n_head):
        to = {"req": me, "head": lax.rem(hd + h, n_head)}
        c = remote(dbuf.at[hd], dbuf.at[hd], d_s.at[h], d_r.at[h], to)
        c.start()
        d_out.append(c)
    for c in c_out:
        c.wait_send()
    for c in fwd:
        c.wait_send()
    loads[3].wait()
    loads[4].wait()
    for h in range(1, n_head):
        src = lax.rem(hd + n_head - h, n_head)
        remote(dbuf.at[src], dbuf.at[src], d_s.at[h], d_r.at[h], {"req": me, "head": lax.rem(hd + h, n_head)}).wait()
    total = dbuf[0].astype(F32)
    for h in range(1, n_head):
        total = total + dbuf[h].astype(F32)
    x = (rf[...] + total).astype(BF)
    xb[...] = x
    rf[...] = x.astype(F32)

    half = NC * rows
    quarter = A * rows
    lines = [lax.rem(a + i, A) for i in range(A)]
    line_from = [lax.rem(a + A - i, A) for i in range(A)]
    cols = [lax.rem(b + i, B) for i in range(B)]
    col_from = [lax.rem(b + B - i, B) for i in range(B)]

    def e1(j):
        return remote(e1s.at[j], e1r.at[j], e1_ss.at[j], e1_rs.at[j], sib)

    def e2(j, i):
        return remote(e2s.at[j, cols[i]], e2r.at[j, i], e2_ss.at[j, i], e2_rs.at[j, i], dev(cols[i] * A + a, core))

    def e3(j, i):
        return remote(e3s.at[j, lines[i]], e3r.at[j, i], e3_ss.at[j, i], e3_rs.at[j, i], dev(b * A + lines[i], core))

    def stage1(j):
        for q in range(4):
            w = wg if q < 2 else wu
            c0 = (q % 2) * (width // 2) + j * cw
            d = lax.dot_general(xb[...], w[:, c0:c0 + cw], NN, preferred_element_type=F32)
            pf[j, q] = d.reshape(CORES, half, cw)
        for q in range(4):
            e1s[j, q] = pf[j, q, 1 - core].astype(BF)
        e1(j).start()

    def stage2(j):
        e1(j).wait()
        for q in range(4):
            e2f[j, :, q] = (pf[j, q, core] + e1r[j, q].astype(F32)).reshape(B, quarter, cw)
        e2s[j] = e2f[j].astype(BF)
        for i in range(1, B):
            e2(j, i).start()

    def stage3(j):
        for i in range(1, B):
            e2(j, i).wait()
        for q in range(4):
            v = e2f[j, b, q]
            for i in range(1, B):
                v = v + e2r[j, i, q].astype(F32)
            for ai in range(A):
                e3f[j, ai, q * rows:(q + 1) * rows, :] = v[ai * rows:(ai + 1) * rows, :]
        e3s[j] = e3f[j].astype(BF)
        for i in range(1, A):
            e3(j, i).start()

    def stage4(j):
        for i in range(1, A):
            e3(j, i).wait()
        v = e3f[j, a]
        for i in range(1, A):
            v = v + e3r[j, i].astype(F32)
        gate = v[:2 * rows]
        up = v[2 * rows:]
        hid = (gate / (1.0 + jnp.exp(-gate)) * up).astype(BF)
        hid_ref[:, j * cw:(j + 1) * cw] = hid[:rows]
        hid_ref[:, width // 2 + j * cw:width // 2 + (j + 1) * cw] = hid[rows:]

    for t in range(jn + 3):
        if t < jn:
            stage1(t)
        if t == 0:
            for pos, nat in enumerate(order):
                rn[nat * rows:(nat + 1) * rows, :] = rf[pos * rows:(pos + 1) * rows, :]
            out_ref[...] = rn[...].astype(BF)
        if 0 <= t - 1 < jn:
            stage2(t - 1)
        if 0 <= t - 2 < jn:
            stage3(t - 2)
        if 0 <= t - 3 < jn:
            stage4(t - 3)


def on_device(n_req, n_head, queries, new_kv, own_kv, man_kv, pages, own_len, resid, w_out, w_gate, w_up):
    A, B = grid_of(n_req)
    NC = A * B
    rows = queries.shape[0]
    kv = new_kv.shape[2] // HD
    blk = rows * GROUP
    pool_t = own_kv.shape[1] * PAGE
    man_t = man_kv.shape[1] * PAGE
    width = w_gate.shape[1]
    cw = 896 if (width // 2) % 896 == 0 else width // 2
    jn = width // 2 // cw
    cols = resid.shape[1]
    all_rows = n_req * rows
    own = own_kv.reshape(2, pool_t, kv * HD)
    man = man_kv.reshape(2, man_t, kv * HD)
    V = pltpu.VMEM
    DMA = pltpu.SemaphoreType.DMA
    vm = pl.BlockSpec(memory_space=pltpu.VMEM)
    sm = pl.BlockSpec(memory_space=pltpu.SMEM)
    hb = pl.BlockSpec(memory_space=pl.ANY)
    quarter = A * rows
    scratch = [
        V((2, pool_t, kv * HD), BF), V(w_out.shape, BF), V(w_gate.shape, BF), V(w_up.shape, BF),
        V((kv * blk, HD), F32), V((NC, kv * blk, HD), BF), V((2, man_t, kv * HD), BF),
        V((blk, pool_t), F32), V((2, kv * blk, HD), F32),
        V((NC, (kv + 1) * blk, HD), BF), V((NC, (kv + 1) * blk, HD), BF),
        V((n_req, kv * blk, HD), BF), V((kv, n_req * blk, HD), F32), V((all_rows, kv * GROUP * HD), BF),
        V((n_head, all_rows, cols), BF), V((all_rows, cols), F32), V((all_rows, cols), F32), V((all_rows, cols), BF),
        V((jn, 4, CORES, NC * rows, cw), F32), V((jn, 4, NC * rows, cw), BF), V((jn, 4, NC * rows, cw), BF),
        V((jn, B, 4, quarter, cw), F32), V((jn, B, 4, quarter, cw), BF), V((jn, B, 4, quarter, cw), BF),
        V((jn, A, 4 * rows, cw), F32), V((jn, A, 4 * rows, cw), BF), V((jn, A, 4 * rows, cw), BF),
        DMA((5,)), DMA, DMA, DMA((NC,)), DMA((NC,)), DMA((NC,)), DMA((NC,)),
        DMA((NC,)), DMA((NC,)), DMA((NC,)), DMA((NC,)), DMA((n_head,)), DMA((n_head,)),
        DMA((jn,)), DMA((jn,)), DMA((jn, B)), DMA((jn, B)), DMA((jn, A)), DMA((jn, A)),
    ]
    return pl.pallas_call(
        functools.partial(kernel, n_req, n_head, jn, cw),
        out_shape=(
            jax.ShapeDtypeStruct((all_rows, cols), BF),
            jax.ShapeDtypeStruct((rows, width), BF),
        ),
        in_specs=[sm, sm, vm, vm, vm, vm, hb, hb, hb, hb],
        out_specs=(vm, vm),
        scratch_shapes=scratch,
        compiler_params=pltpu.CompilerParams(
            collective_id=0, has_side_effects=True, vmem_limit_bytes=58 * 1024 * 1024
        ),
        name="decode_layer",
    )(pages, own_len, queries, new_kv, man, resid, own, w_out, w_gate, w_up)


def solution(mesh):
    in_specs = (
        P("req", "head"),
        P(None, "req", "head"),
        P(None, "req", None, "head"),
        P(None, "req", None, "head"),
        P("req", None),
        P("req"),
        P(None, "req"),
        P("head", "req"),
        P("req", "head"),
        P("req", "head"),
    )
    out_specs = (P(None, "req"), P("req", "head"))
    return jax.shard_map(
        functools.partial(on_device, mesh.shape["req"], mesh.shape["head"]),
        mesh=mesh, in_specs=in_specs, out_specs=out_specs, check_vma=False,
    )
```

```python
import functools

import jax
import jax.numpy as jnp
from jax import lax
from jax.experimental import pallas as pl
from jax.experimental.pallas import tpu as pltpu
from jax.sharding import PartitionSpec as P

HD = 128
PAGE = 64
MAXP = 8
GROUP = 8
CORES = 2
BF = jnp.bfloat16
F32 = jnp.float32
NT = (((1,), (1,)), ((), ()))
NN = (((1,), (0,)), ((), ()))


def grid_of(n_req):
    chips = n_req // CORES
    b = 1
    while b * 2 * b * 2 <= chips:
        b *= 2
    while chips % b:
        b -= 1
    return chips // b, b


def kernel(
    n_req, n_head, jn, cw,
    pages, own_len, queries, new_kv, man, res_hbm, own_hbm, wo_hbm, wg_hbm, wu_hbm,
    out_ref, hid_ref,
    pool, wo, wg, wu, qf, qbuf, kvb, resid, bias, nf, sbuf, rbuf, abuf, af, amat, dbuf,
    rf, rn, xb, pf, e1s, e1r, e2f, e2s, e2r, e3f, e3s, e3r,
    lsem, kv_s, kv_r, kf_s, kf_r, q_s, q_r, p_s, p_r, c_s, c_r, y_s, y_r, f_s, f_r, d_s, d_r,
    e1_ss, e1_rs, e2_ss, e2_rs, e3_ss, e3_rs,
):
    A, B = grid_of(n_req)
    NC = A * B
    kv = man.shape[2] // HD
    rows = queries.shape[0]
    blk = rows * GROUP
    width = wg.shape[1]
    scale = HD ** (-0.5)

    me = lax.axis_index("req")
    hd = lax.axis_index("head")
    core = lax.rem(me, CORES)
    chip = me // CORES
    a = chip // B
    b = lax.rem(chip, B)
    cp = b * A + a

    def dev(cp_, core_):
        return {"req": (lax.rem(cp_, A) * B + cp_ // A) * CORES + core_, "head": hd}

    def remote(src, dst, ss, rs, to):
        return pltpu.make_async_remote_copy(
            src_ref=src, dst_ref=dst, send_sem=ss, recv_sem=rs,
            device_id=to, device_id_type=pl.DeviceIdType.MESH,
        )

    sib = dev(cp, 1 - core)
    lines = [lax.rem(a + i, A) for i in range(A)]
    line_from = [lax.rem(a + A - i, A) for i in range(A)]
    cols = [lax.rem(b + i, B) for i in range(B)]
    col_from = [lax.rem(b + B - i, B) for i in range(B)]
    line_dev = [dev(b * A + lines[i], core) for i in range(A)]
    col_dev = [dev(cols[i] * A + a, core) for i in range(B)]
    parts = [(0, kv // 2), (kv // 2, kv)] if kv > 1 else [(0, kv)]
    np_ = len(parts)

    barrier = pltpu.get_barrier_semaphore()

    def greet(to):
        pl.semaphore_signal(barrier, inc=1, device_id=to, device_id_type=pl.DeviceIdType.MESH)

    greet(sib)
    for i in range(1, A):
        greet(line_dev[i])
    for i in range(1, B):
        greet(col_dev[i])
    for h in range(1, n_head):
        greet({"req": me, "head": lax.rem(hd + h, n_head)})

    loads = [
        pltpu.make_async_copy(own_hbm.at[0], pool.at[0], lsem.at[0]),
        pltpu.make_async_copy(own_hbm.at[1], pool.at[1], lsem.at[1]),
        pltpu.make_async_copy(wo_hbm, wo, lsem.at[2]),
        pltpu.make_async_copy(wg_hbm, wg, lsem.at[3]),
        pltpu.make_async_copy(wu_hbm, wu, lsem.at[4]),
        pltpu.make_async_copy(man, kvb.at[b, core], lsem.at[5]),
        pltpu.make_async_copy(res_hbm, resid, lsem.at[6]),
    ]
    loads[0].start()
    loads[1].start()

    qv = queries[...].astype(F32)
    for k in range(kv):
        for g in range(GROUP):
            lane = (k * GROUP + g) * HD
            qf[pl.ds(k * blk + g, rows, stride=GROUP), :] = qv[:, lane:lane + HD]
    qbuf[a] = qf[...].astype(BF)

    pl.semaphore_wait(barrier, 1 + (A - 1) + (B - 1) + (n_head - 1))

    def kv_col(t, i):
        return remote(man.at[t], kvb.at[b, core, t], kv_s.at[t, i], kv_r.at[t, i], col_dev[i])

    def kv_sib(t, i):
        src = man.at[t] if i == 0 else kvb.at[col_from[i], core, t]
        return remote(src, kvb.at[col_from[i], core, t], kf_s.at[t, i], kf_r.at[t, i], sib)

    def q_line(i):
        return remote(qbuf.at[a], qbuf.at[a], q_s.at[i], q_r.at[i], line_dev[i])

    for i in range(1, B):
        kv_col(0, i).start()
    for i in range(1, A):
        q_line(i).start()
    for i in range(1, B):
        kv_col(1, i).start()
    kv_sib(0, 0).start()
    kv_sib(1, 0).start()
    loads[5].start()
    loads[6].start()

    def kv_forward(t):
        for i in range(1, B):
            kv_col(t, i).wait_send()
            got = kvb.at[col_from[i], core, t]
            remote(got, got, kv_s.at[t, i], kv_r.at[t, i], col_dev[i]).wait_recv()
            kv_sib(t, i).start()

    toks = pool.shape[1]
    tok_page = lax.broadcasted_iota(jnp.int32, (GROUP, toks), 1) // PAGE
    for r in range(rows):
        cnt = jnp.zeros((GROUP, toks), F32)
        for i in range(MAXP):
            pid = jnp.where(i < own_len[r], pages[r, i], -1)
            cnt = cnt + jnp.where(tok_page == pid, 1.0, 0.0)
        bias[r * GROUP:(r + 1) * GROUP, :] = jnp.where(cnt > 0.0, jnp.log(jnp.maximum(cnt, 1.0)), -1e30)
    for t in range(2):
        nv = new_kv[t].astype(F32)
        for k in range(kv):
            for g in range(GROUP):
                nf[t, pl.ds(k * blk + g, rows, stride=GROUP), :] = nv[:, k * HD:(k + 1) * HD]
    loads[0].wait()
    loads[1].wait()
    for c in loads[2:5]:
        c.start()
    own = []
    for k in range(kv):
        rs = slice(k * blk, (k + 1) * blk)
        ls = slice(k * HD, (k + 1) * HD)
        s = lax.dot_general(qf[rs].astype(BF), pool[0, :, ls], NT, preferred_element_type=F32) * scale + bias[...]
        s_new = jnp.sum(qf[rs] * nf[0, rs], axis=1, keepdims=True) * scale
        m = jnp.maximum(jnp.max(s, axis=1, keepdims=True), s_new)
        p = jnp.exp(s - m)
        e_new = jnp.exp(s_new - m)
        l = jnp.sum(p, axis=1, keepdims=True) + e_new
        acc = lax.dot_general(p.astype(BF), pool[1, :, ls], NN, preferred_element_type=F32)
        acc = acc + e_new.astype(BF).astype(F32) * nf[1, rs]
        own.append((m, l, acc))
        if k == (kv - 1) // 2:
            kv_forward(0)
    kv_forward(1)

    loads[5].wait()
    for i in range(1, A):
        q_line(i).wait_send()
        got = qbuf.at[line_from[i]]
        remote(got, got, q_s.at[i], q_r.at[i], line_dev[i]).wait_recv()
    for t in range(2):
        for i in range(B):
            kv_sib(t, i).wait_send()
            got = kvb.at[col_from[i], 1 - core, t]
            remote(got, got, kf_s.at[t, i], kf_r.at[t, i], sib).wait_recv()
    mrows = A * blk
    mtoks = B * CORES * kvb.shape[3]
    lane = lax.broadcasted_iota(jnp.int32, (mrows, HD), 1)
    stats = jnp.zeros((mrows, HD), F32)

    def p_line(n, i):
        r0, r1 = parts[n][0] * blk, parts[n][1] * blk + (blk if n == np_ - 1 else 0)
        return remote(
            sbuf.at[lines[i], r0:r1], rbuf.at[a, r0:r1], p_s.at[n, i], p_r.at[n, i], line_dev[i]
        )

    def p_wait(n, i):
        r0, r1 = parts[n][0] * blk, parts[n][1] * blk + (blk if n == np_ - 1 else 0)
        p_line(n, i).wait_send()
        got = rbuf.at[line_from[i], r0:r1]
        remote(got, got, p_s.at[n, i], p_r.at[n, i], line_dev[i]).wait_recv()

    for n, (k0, k1) in enumerate(parts):
        for k in range(k0, k1):
            ls = slice(k * HD, (k + 1) * HD)
            q = qbuf[:, k * blk:(k + 1) * blk, :].reshape(mrows, HD)
            keys = kvb[:, :, 0, :, ls].reshape(mtoks, HD)
            vals = kvb[:, :, 1, :, ls].reshape(mtoks, HD)
            s = lax.dot_general(q, keys, NT, preferred_element_type=F32) * scale
            m = jnp.max(s, axis=1, keepdims=True).astype(BF).astype(F32)
            p = jnp.exp(s - m)
            l = jnp.sum(p, axis=1, keepdims=True)
            acc = lax.dot_general(p.astype(BF), vals, NN, preferred_element_type=F32)
            sbuf[:, k * blk:(k + 1) * blk, :] = acc.astype(BF).reshape(A, blk, HD)
            l_hi = l.astype(BF).astype(F32)
            stats = jnp.where(lane == k, m, stats)
            stats = jnp.where(lane == kv + k, l_hi, stats)
            stats = jnp.where(lane == 2 * kv + k, l - l_hi, stats)
        if n == np_ - 1:
            sbuf[:, kv * blk:(kv + 1) * blk, :] = stats.astype(BF).reshape(A, blk, HD)
        for i in range(1, A):
            p_line(n, i).start()
    rbuf[a] = sbuf[a]
    for n in range(np_):
        for i in range(1, A):
            p_wait(n, i)

    st = [rbuf[n, kv * blk:(kv + 1) * blk, :].astype(F32) for n in range(A)]
    mine = core * NC + cp
    sends = []

    def push(n, slot, ss, rs, to):
        ref = abuf.at[slot, parts[n][0] * blk:parts[n][1] * blk]
        c = remote(ref, ref, ss, rs, to)
        c.start()
        sends.append(c)

    def landed(n, slot, ss, rs, to):
        ref = abuf.at[slot, parts[n][0] * blk:parts[n][1] * blk]
        remote(ref, ref, ss, rs, to).wait_recv()

    def slot_of(core_, ib, ia):
        return core_ * NC + col_from[ib] * A + line_from[ia]

    for n, (k0, k1) in enumerate(parts):
        for k in range(k0, k1):
            rs = slice(k * blk, (k + 1) * blk)
            m, l, acc = own[k]
            top = m
            for i in range(A):
                top = jnp.maximum(top, st[i][:, k:k + 1])
            f = jnp.exp(m - top)
            l = l * f
            acc = acc * f
            for i in range(A):
                f = jnp.exp(st[i][:, k:k + 1] - top)
                l = l + f * (st[i][:, kv + k:kv + k + 1] + st[i][:, 2 * kv + k:2 * kv + k + 1])
                acc = acc + f * rbuf[i, rs, :].astype(F32)
            abuf[mine, rs, :] = (acc / l).astype(BF)
        for i in range(1, A):
            push(n, mine, c_s.at[n, i], c_r.at[n, i], line_dev[i])
        for i in range(1, B):
            push(n, mine, y_s.at[n, i, 0], y_r.at[n, i, 0], col_dev[i])
        push(n, mine, f_s.at[n, 0, 0], f_r.at[n, 0, 0], sib)
    for n in range(np_):
        for ia in range(1, A):
            slot = slot_of(core, 0, ia)
            landed(n, slot, c_s.at[n, ia], c_r.at[n, ia], line_dev[ia])
            for ib in range(1, B):
                push(n, slot, y_s.at[n, ib, ia], y_r.at[n, ib, ia], col_dev[ib])
            push(n, slot, f_s.at[n, 0, ia], f_r.at[n, 0, ia], sib)
    for n in range(np_):
        for ib in range(1, B):
            for ia in range(A):
                slot = slot_of(core, ib, ia)
                landed(n, slot, y_s.at[n, ib, ia], y_r.at[n, ib, ia], col_dev[ib])
                push(n, slot, f_s.at[n, ib, ia], f_r.at[n, ib, ia], sib)

    loads[6].wait()
    rv = resid[...].astype(F32)
    order = [(ai * B + bi) * CORES + ci for ci in range(CORES) for bi in range(B) for ai in range(A)]
    for pos, nat in enumerate(order):
        rf[pos * rows:(pos + 1) * rows, :] = rv[nat * rows:(nat + 1) * rows, :]

    all_rows = n_req * rows
    loads[2].wait()
    part = None
    for n, (k0, k1) in enumerate(parts):
        for ib in range(B):
            for ia in range(A):
                landed(n, slot_of(1 - core, ib, ia), f_s.at[n, ib, ia], f_r.at[n, ib, ia], sib)
        for k in range(k0, k1):
            af[k] = abuf[:, k * blk:(k + 1) * blk, :].astype(F32).reshape(n_req * blk, HD)
        for k in range(k0, k1):
            for g in range(GROUP):
                lane0 = (k * GROUP + g) * HD
                amat[:, lane0:lane0 + HD] = af[k, pl.ds(g, all_rows, stride=GROUP), :].astype(BF)
        ks = slice(k0 * GROUP * HD, k1 * GROUP * HD)
        d = lax.dot_general(amat[:, ks], wo[ks], NN, preferred_element_type=F32)
        part = d if part is None else part + d
    dbuf[hd] = part.astype(BF)
    d_out = []
    for h in range(1, n_head):
        to = {"req": me, "head": lax.rem(hd + h, n_head)}
        c = remote(dbuf.at[hd], dbuf.at[hd], d_s.at[h], d_r.at[h], to)
        c.start()
        d_out.append(c)
    for c in sends:
        c.wait_send()
    loads[3].wait()
    loads[4].wait()
    for h in range(1, n_head):
        src = lax.rem(hd + n_head - h, n_head)
        remote(dbuf.at[src], dbuf.at[src], d_s.at[h], d_r.at[h], {"req": me, "head": lax.rem(hd + h, n_head)}).wait()
    total = dbuf[0].astype(F32)
    for h in range(1, n_head):
        total = total + dbuf[h].astype(F32)
    x = (rf[...] + total).astype(BF)
    xb[...] = x
    rf[...] = x.astype(F32)

    half = NC * rows
    quarter = A * rows
    def e1(j):
        return remote(e1s.at[j], e1r.at[j], e1_ss.at[j], e1_rs.at[j], sib)

    def e2(j, i):
        return remote(e2s.at[j, cols[i]], e2r.at[j, i], e2_ss.at[j, i], e2_rs.at[j, i], dev(cols[i] * A + a, core))

    def e3(j, i):
        return remote(e3s.at[j, lines[i]], e3r.at[j, i], e3_ss.at[j, i], e3_rs.at[j, i], dev(b * A + lines[i], core))

    def stage1(j):
        for q in range(4):
            w = wg if q < 2 else wu
            c0 = (q % 2) * (width // 2) + j * cw
            d = lax.dot_general(xb[...], w[:, c0:c0 + cw], NN, preferred_element_type=F32)
            pf[j, q] = d.reshape(CORES, half, cw)
        for q in range(4):
            e1s[j, q] = pf[j, q, 1 - core].astype(BF)
        e1(j).start()

    def stage2(j):
        e1(j).wait()
        for q in range(4):
            e2f[j, :, q] = (pf[j, q, core] + e1r[j, q].astype(F32)).reshape(B, quarter, cw)
        e2s[j] = e2f[j].astype(BF)
        for i in range(1, B):
            e2(j, i).start()

    def stage3(j):
        for i in range(1, B):
            e2(j, i).wait()
        for q in range(4):
            v = e2f[j, b, q]
            for i in range(1, B):
                v = v + e2r[j, i, q].astype(F32)
            for ai in range(A):
                e3f[j, ai, q * rows:(q + 1) * rows, :] = v[ai * rows:(ai + 1) * rows, :]
        e3s[j] = e3f[j].astype(BF)
        for i in range(1, A):
            e3(j, i).start()

    def stage4(j):
        for i in range(1, A):
            e3(j, i).wait()
        v = e3f[j, a]
        for i in range(1, A):
            v = v + e3r[j, i].astype(F32)
        gate = v[:2 * rows]
        up = v[2 * rows:]
        hid = (gate / (1.0 + jnp.exp(-gate)) * up).astype(BF)
        hid_ref[:, j * cw:(j + 1) * cw] = hid[:rows]
        hid_ref[:, width // 2 + j * cw:width // 2 + (j + 1) * cw] = hid[rows:]

    for t in range(jn + 3):
        if t < jn:
            stage1(t)
        if t == 0:
            for pos, nat in enumerate(order):
                rn[nat * rows:(nat + 1) * rows, :] = rf[pos * rows:(pos + 1) * rows, :]
            out_ref[...] = rn[...].astype(BF)
        if 0 <= t - 1 < jn:
            stage2(t - 1)
        if 0 <= t - 2 < jn:
            stage3(t - 2)
        if 0 <= t - 3 < jn:
            stage4(t - 3)


def on_device(n_req, n_head, queries, new_kv, own_kv, man_kv, pages, own_len, resid, w_out, w_gate, w_up):
    A, B = grid_of(n_req)
    NC = A * B
    rows = queries.shape[0]
    kv = new_kv.shape[2] // HD
    blk = rows * GROUP
    pool_t = own_kv.shape[1] * PAGE
    man_t = man_kv.shape[1] * PAGE
    width = w_gate.shape[1]
    cw = 896 if (width // 2) % 896 == 0 else width // 2
    jn = width // 2 // cw
    cols = resid.shape[1]
    all_rows = n_req * rows
    own = own_kv.reshape(2, pool_t, kv * HD)
    man = man_kv.reshape(2, man_t, kv * HD)
    V = pltpu.VMEM
    DMA = pltpu.SemaphoreType.DMA
    vm = pl.BlockSpec(memory_space=pltpu.VMEM)
    sm = pl.BlockSpec(memory_space=pltpu.SMEM)
    hb = pl.BlockSpec(memory_space=pl.ANY)
    quarter = A * rows
    np_ = 2 if kv > 1 else 1
    scratch = [
        V((2, pool_t, kv * HD), BF), V(w_out.shape, BF), V(w_gate.shape, BF), V(w_up.shape, BF),
        V((kv * blk, HD), F32), V((A, kv * blk, HD), BF), V((B, CORES, 2, man_t, kv * HD), BF), V((all_rows, cols), BF),
        V((blk, pool_t), F32), V((2, kv * blk, HD), F32),
        V((A, (kv + 1) * blk, HD), BF), V((A, (kv + 1) * blk, HD), BF),
        V((n_req, kv * blk, HD), BF), V((kv, n_req * blk, HD), F32), V((all_rows, kv * GROUP * HD), BF),
        V((n_head, all_rows, cols), BF), V((all_rows, cols), F32), V((all_rows, cols), F32), V((all_rows, cols), BF),
        V((jn, 4, CORES, NC * rows, cw), F32), V((jn, 4, NC * rows, cw), BF), V((jn, 4, NC * rows, cw), BF),
        V((jn, B, 4, quarter, cw), F32), V((jn, B, 4, quarter, cw), BF), V((jn, B, 4, quarter, cw), BF),
        V((jn, A, 4 * rows, cw), F32), V((jn, A, 4 * rows, cw), BF), V((jn, A, 4 * rows, cw), BF),
        DMA((7,)), DMA((2, B)), DMA((2, B)), DMA((2, B)), DMA((2, B)), DMA((A,)), DMA((A,)),
        DMA((np_, A)), DMA((np_, A)), DMA((np_, A)), DMA((np_, A)),
        DMA((np_, B, A)), DMA((np_, B, A)), DMA((np_, B, A)), DMA((np_, B, A)), DMA((n_head,)), DMA((n_head,)),
        DMA((jn,)), DMA((jn,)), DMA((jn, B)), DMA((jn, B)), DMA((jn, A)), DMA((jn, A)),
    ]
    return pl.pallas_call(
        functools.partial(kernel, n_req, n_head, jn, cw),
        out_shape=(
            jax.ShapeDtypeStruct((all_rows, cols), BF),
            jax.ShapeDtypeStruct((rows, width), BF),
        ),
        in_specs=[sm, sm, vm, vm, hb, hb, hb, hb, hb, hb],
        out_specs=(vm, vm),
        scratch_shapes=scratch,
        compiler_params=pltpu.CompilerParams(
            collective_id=0, has_side_effects=True, vmem_limit_bytes=58 * 1024 * 1024
        ),
        name="decode_layer",
    )(pages, own_len, queries, new_kv, man, resid, own, w_out, w_gate, w_up)


def solution(mesh):
    in_specs = (
        P("req", "head"),
        P(None, "req", "head"),
        P(None, "req", None, "head"),
        P(None, "req", None, "head"),
        P("req", None),
        P("req"),
        P(None, "req"),
        P("head", "req"),
        P("req", "head"),
        P("req", "head"),
    )
    out_specs = (P(None, "req"), P("req", "head"))
    return jax.shard_map(
        functools.partial(on_device, mesh.shape["req"], mesh.shape["head"]),
        mesh=mesh, in_specs=in_specs, out_specs=out_specs, check_vma=False,
    )
```
